512 devices in a mesh: ev: 64 (over x, z, core), st: 8 (over y).
Axes of the slice: x: 4, y: 8, z: 8, core: 2. Of those that a mesh axis runs over, the one named last changes fastest.
Arguments:
- waveforms: bfloat16 [2048, 32, 3, 2048], P(('ev', 'st'))
- pair_list: int32 [64, 64, 3], P('ev'), may hold values from 0 to 31, as said below
- pair_count: int32 [64], P('ev'), may hold values from 1 to 64, as said below
Outputs:
- correlation: float32 [4096, 32, 3, 256], P('ev', 'st')
The draws below stay inside these ranges and needn't reach their ends.
Inputs may be any that keep to these rules, and one draw needn't show every extreme that they name: `pair_list`: each entry holds an event number of 0 to 31 in its first and third place and a block offset o of 0 to 2 in its second, with b + o < 64 for block b; when o is 0 the two events differ. Slots from pair_count onward hold the same law and are ignored. `pair_count`: some block has all 64 slots live in every draw; loads differ widely between blocks.
All inputs are finite; a program needn't handle non-finite values.
Results may differ from the reference program's by a relative error of at most 0.0047.
Values may be sent and summed in bfloat16 or wider, within the bound.
A program may use at most 64 MiB of HBM per device.

```python
import math
import jax
import jax.numpy as jnp
from jax import lax

WIN = 2048
NFFT = 4096
FREQS = 2048
STATIONS = 32
COMP = 3
LAG = 128
REACH = 2
E_DEV = 32
P_DEV = 64
BLOCKS = 64
EVENTS = 2048
PAIRS = 4096


def draw_waveforms(key, part):
    key = jax.random.fold_in(key, 5)
    amp_key, noise_key = jax.random.split(key, 2)
    amplitude = jnp.exp(jax.random.uniform(amp_key, (EVENTS, STATIONS, COMP, 1), jnp.float32, 0.0, 2.302585))
    noise = jnp.clip(jax.random.normal(noise_key, (EVENTS, STATIONS, COMP, WIN), jnp.float32), -6.0, 6.0)
    values = amplitude * noise
    return values.astype(jnp.bfloat16)


def draw_pair_list(key, part):
    key = jax.random.fold_in(key, 11)
    offset_key, first_key, other_key, shift_key = jax.random.split(key, 4)
    block_ids = lax.broadcasted_iota(jnp.int32, (BLOCKS, P_DEV), 0)
    room = jnp.minimum(REACH, BLOCKS - 1 - block_ids)
    block_offset = jax.random.randint(offset_key, (BLOCKS, P_DEV), 0, REACH + 1) % (room + 1)
    first_event = jax.random.randint(first_key, (BLOCKS, P_DEV), 0, E_DEV)
    other_event = jax.random.randint(other_key, (BLOCKS, P_DEV), 0, E_DEV)
    moved = jax.random.randint(shift_key, (BLOCKS, P_DEV), 1, E_DEV)
    second_event = jnp.where(block_offset == 0, (first_event + moved) % E_DEV, other_event)
    return jnp.stack([first_event, block_offset, second_event], axis=2).astype(jnp.int32)


def draw_pair_count(key, part):
    key = jax.random.fold_in(key, 17)
    phase_key, load_key = jax.random.split(key, 2)
    phase_shift = jax.random.randint(phase_key, (), 0, 4)
    block_ids = jnp.arange(BLOCKS, dtype=jnp.int32)
    full_block = (block_ids + phase_shift) % 4 == 0
    partial_value = jax.random.randint(load_key, (BLOCKS,), max(1, P_DEV // 8), P_DEV // 2 + 1)
    return jnp.where(full_block, P_DEV, partial_value).astype(jnp.int32)


def setup_inputs(seed: int = 0) -> dict:
    streams_of = jax.random.split(jax.random.key(seed), 4)
    return {
        "waveforms": draw_waveforms(jax.random.fold_in(streams_of[3], 71), 0),
        "pair_list": draw_pair_list(jax.random.fold_in(streams_of[3], 71), 0),
        "pair_count": draw_pair_count(jax.random.fold_in(streams_of[3], 71), 0),
    }


def forward_table():
    sample_ids = jnp.arange(WIN, dtype=jnp.int32)[:, None]
    frequency = jnp.arange(FREQS, dtype=jnp.int32)[None, :]
    phases = sample_ids * frequency % NFFT
    angles = phases.astype(jnp.float32) * (2.0 * math.pi / NFFT)
    return jnp.concatenate([jnp.cos(angles), -jnp.sin(angles)], axis=1).astype(jnp.bfloat16)

def lag_tables():
    frequency = jnp.arange(FREQS, dtype=jnp.int32)[:, None]
    lag_ids = jnp.arange(2 * LAG, dtype=jnp.int32)[None, :] - LAG + NFFT
    phases = frequency * lag_ids % NFFT
    angles = phases.astype(jnp.float32) * (2.0 * math.pi / NFFT)
    weight = jnp.where(frequency == 0, 1.0, 2.0) * (math.sqrt(WIN) / NFFT)
    lag_cos = (weight * jnp.cos(angles)).astype(jnp.bfloat16)
    lag_sin = (-weight * jnp.sin(angles)).astype(jnp.bfloat16)
    return (lag_cos, lag_sin)

def block_spectra(windows, dft_table):
    flat_rows = windows.reshape(-1, WIN)
    squares = lax.optimization_barrier(jnp.mean(jnp.square(flat_rows.astype(jnp.float32)), axis=1))
    scaling = 1.0 / jnp.sqrt(WIN * (squares + 1e-06))
    product = jnp.dot(flat_rows, dft_table, preferred_element_type=jnp.float32) * scaling[:, None]
    return product.astype(jnp.bfloat16).reshape(E_DEV, STATIONS, COMP, 2, FREQS)

def reference(waveforms, pair_list, pair_count):
    dft_table = forward_table()
    grouped = waveforms.reshape(BLOCKS, E_DEV, STATIONS, COMP, WIN)
    spectra = lax.map(lambda windows: block_spectra(windows, dft_table), grouped)
    lag_cos, lag_sin = lag_tables()

    def one_block(packed):
        block_id, slots, live_count = packed
        first_event = slots[:, 0]
        block_offset = slots[:, 1]
        second_event = slots[:, 2]
        partner = jnp.minimum(block_id + block_offset, BLOCKS - 1).astype(jnp.int32)
        first_spec = spectra[block_id][first_event]
        second_spec = spectra[partner, second_event]
        left_real = first_spec[..., 0, :].astype(jnp.float32)
        left_imag = first_spec[..., 1, :].astype(jnp.float32)
        right_real = second_spec[..., 0, :].astype(jnp.float32)
        right_imag = second_spec[..., 1, :].astype(jnp.float32)
        cross_real = (left_real * right_real + left_imag * right_imag).astype(jnp.bfloat16)
        cross_imag = (left_imag * right_real - left_real * right_imag).astype(jnp.bfloat16)
        lagged = jnp.dot(cross_real.reshape(-1, FREQS), lag_cos, preferred_element_type=jnp.float32)
        lagged = lagged + jnp.dot(cross_imag.reshape(-1, FREQS), lag_sin, preferred_element_type=jnp.float32)
        lagged = lagged.reshape(P_DEV, STATIONS, COMP, 2 * LAG)
        live_slots = jnp.arange(P_DEV, dtype=jnp.int32) < live_count
        return jnp.where(live_slots[:, None, None, None], lagged, jnp.zeros_like(lagged))
    result = lax.map(one_block, (jnp.arange(BLOCKS, dtype=jnp.int32), pair_list, pair_count))
    return result.reshape(PAIRS, STATIONS, COMP, 2 * LAG)
```

```python
import math

import jax
import jax.numpy as jnp
import numpy as np
from jax import lax
from jax.experimental import pallas as pl
from jax.experimental.pallas import tpu as pltpu
from jax.sharding import PartitionSpec as P

MESH = pl.DeviceIdType.MESH
EV, ST = 64, 8
EVENTS, OWN, STATIONS, COMP, WIN = 32, 4, 4, 3, 2048
PAIRS, LAGS = 64, 256
HALF, CHUNK, SIZE = 1024, 256, 512
STEPS = HALF // CHUNK
ROWS = EVENTS * 8
PART = OWN * 8
PIECES = 2 * COMP
WINDOW = 2
ORDER = (4, 3, 5, 2, 6, 1, 7)
ARRIVAL = (1, 7, 2, 6, 3, 5, 4)


def tables():
    sample = np.arange(SIZE)[:, None]
    odd = 2 * np.arange(SIZE // 2)[None, :] + 1
    angle = (sample * odd % (2 * SIZE)) * (math.pi / SIZE)
    forward = np.concatenate([np.cos(angle), -np.sin(angle)], axis=1)
    weight = 2.0 / SIZE * math.sqrt(WIN)
    back = weight * forward[:LAGS].T
    return jnp.asarray(forward, jnp.bfloat16), jnp.asarray(back, jnp.bfloat16)


def upper(shape, axis):
    return lax.broadcasted_iota(jnp.int32, shape, axis) < 4


def swap_halves(value):
    return pltpu.roll(value, 4, 1)


def kernel(
    slots_ref, count_ref, wave_ref, forward_hbm, back_hbm, out_ref,
    forward_ref, back_ref, raw, parts, held, wide, first_spec, second_spec, nyquist, scales, adder, cross, rank_one,
    table_sem, raw_sem, own_sem, y_send, y_recv, z_send, z_recv, s_send, s_recv,
):
    ev = lax.axis_index("ev")
    st = lax.axis_index("st")
    core = lax.rem(ev, 2)
    earlier = lax.rem(ev + EV - 2, EV)
    later = lax.rem(ev + 2, EV)
    sibling = ev + 1 - 2 * core

    raw_copies = []
    for c in range(COMP):
        copy = pltpu.make_async_copy(wave_ref.at[:, c], raw.at[:, c], raw_sem.at[c])
        copy.start()
        raw_copies.append(copy)
    table_copies = [
        pltpu.make_async_copy(forward_hbm, forward_ref, table_sem.at[0]),
        pltpu.make_async_copy(back_hbm, back_ref, table_sem.at[1]),
    ]
    for copy in table_copies:
        copy.start()

    barrier = pltpu.get_barrier_semaphore()
    for by in range(1, ST):
        pl.semaphore_signal(
            barrier, inc=1, device_id=(ev, lax.rem(st + by, ST)), device_id_type=MESH
        )
    for other in (earlier, later, sibling):
        pl.semaphore_signal(barrier, inc=1, device_id=(other, st), device_id_type=MESH)

    def place(n, source):
        half = n % 2 * 16
        return n // 2, pl.ds(pl.multiple_of(source * PART + half, 16), 16), slice(half, half + 16)

    def y_copy(n, by):
        target = lax.rem(st + by, ST)
        c, rows, half = place(n, st)
        return pltpu.make_async_remote_copy(
            src_ref=parts.at[c, target, half],
            dst_ref=held.at[0, c, rows],
            send_sem=y_send.at[n, by],
            recv_sem=y_recv.at[n, by],
            device_id=(ev, target),
            device_id_type=MESH,
        )

    def own_copy(n):
        c, rows, half = place(n, st)
        return pltpu.make_async_copy(parts.at[c, st, half], held.at[0, c, rows], own_sem.at[n])

    def z_copy(n, by):
        c, rows, _ = place(n, lax.rem(st + ST - by, ST))
        return pltpu.make_async_remote_copy(
            src_ref=held.at[0, c, rows],
            dst_ref=held.at[2, c, rows],
            send_sem=z_send.at[n, by],
            recv_sem=z_recv.at[n, by],
            device_id=(earlier, st),
            device_id_type=MESH,
        )

    def sibling_copy(n, by):
        c, rows, _ = place(n, lax.rem(st + ST - by, ST))
        return pltpu.make_async_remote_copy(
            src_ref=held.at[2 - 2 * core, c, rows],
            dst_ref=held.at[1, c, rows],
            send_sem=s_send.at[n, by],
            recv_sem=s_recv.at[n, by],
            device_id=(sibling, st),
            device_id_type=MESH,
        )

    def lay_out(c):
        def group(g, carry):
            stations = pl.ds(pl.multiple_of(g * 16, 16), 16)
            for pair in range(OWN // 2):
                for piece in range(HALF // 256):
                    low = slice(piece * 256, piece * 256 + 256)
                    high = slice(HALF + piece * 256, HALF + piece * 256 + 256)
                    made = [[], [], [], []]
                    for e in (2 * pair, 2 * pair + 1):
                        head = raw[e, c, stations, low].astype(jnp.float32)
                        tail = raw[e, c, stations, high].astype(jnp.float32)
                        for t in range(2):
                            h0 = head[8 * t : 8 * t + 8]
                            h1 = tail[8 * t : 8 * t + 8]
                            top = upper(h0.shape, 0)
                            made[2 * t].append(jnp.where(top, h0, pltpu.roll(h1, 4, 0)))
                            made[2 * t + 1].append(jnp.where(top, pltpu.roll(h0, 4, 0), h1))
                    for d in range(4):
                        both = jnp.concatenate(made[d], axis=0).astype(jnp.bfloat16)
                        parts[c, 4 * g + d, 16 * pair : 16 * pair + 16, low] = both
            return carry

        lax.fori_loop(0, 2, group, 0)

    def measure(c, block):
        energy = jnp.zeros((ROWS, 128), jnp.float32)
        total = jnp.zeros((ROWS, 128), jnp.float32)
        for piece in range(HALF // 128):
            x = held[block, c, :, 128 * piece : 128 * piece + 128].astype(jnp.float32)
            energy = energy + x * x
            total = total + x
        split = []
        for value in (energy, total):
            high = value.astype(jnp.bfloat16)
            wide_high = high.astype(jnp.float32)
            rest = jnp.where(jnp.abs(wide_high) < jnp.inf, value - wide_high, 0.0)
            split += [high, rest.astype(jnp.bfloat16)]
        sums = jnp.dot(
            jnp.concatenate(split, axis=1), adder[...], preferred_element_type=jnp.float32
        ).reshape(EVENTS, 8, 256)
        sums = sums + swap_halves(sums)
        scale = 1.0 / jnp.sqrt(WIN * (sums[:, :, :128] * (1.0 / WIN) + 1e-6))
        scales[block] = scale
        nyquist[pl.ds(block * EVENTS, EVENTS)] = sums[:, :, 128:] * scale

    def scaled(product, block):
        product = product.reshape(EVENTS, 8, SIZE)
        scale = scales[block]
        return jnp.concatenate(
            [product[:, :, 128 * n : 128 * n + 128] * scale for n in range(SIZE // 128)], axis=2
        )

    def transform_first(c):
        x = held[0, c]
        head = swap_halves(x[:, :128].astype(jnp.float32).reshape(EVENTS, 8, 128))
        tail = swap_halves(x[:, HALF - 128 :].astype(jnp.float32).reshape(EVENTS, 8, 128))
        top = upper(head.shape, 1)
        before = jnp.where(top, 0.0, tail).reshape(ROWS, 128).astype(jnp.bfloat16)
        after = jnp.where(top, head, 0.0).reshape(ROWS, 128).astype(jnp.bfloat16)
        wide[:, :128] = before
        wide[:, 128 : 128 + HALF] = x
        wide[:, 128 + HALF :] = after
        for q in range(STEPS):
            product = jnp.dot(
                wide[:, CHUNK * q : CHUNK * q + SIZE],
                forward_ref[...],
                preferred_element_type=jnp.float32,
            )
            first_spec[:, q] = scaled(product, 0)

    def transform_second(c, block):
        for q in range(STEPS):
            product = jnp.dot(
                held[block, c, :, CHUNK * q : CHUNK * q + CHUNK],
                forward_ref[:CHUNK, :],
                preferred_element_type=jnp.float32,
            )
            second_spec[pl.ds(block * EVENTS, EVENTS), q] = scaled(product, block)

    def correlate(c):
        def one(p):
            first = slots_ref[0, 0, p]
            second = slots_ref[1, 0, p] * EVENTS + slots_ref[2, 0, p]
            real = jnp.zeros((8, SIZE // 2), jnp.float32)
            imag = jnp.zeros((8, SIZE // 2), jnp.float32)
            for q in range(STEPS):
                a = first_spec[first, q]
                b = second_spec[second, q]
                ar, ai = a[:, : SIZE // 2], a[:, SIZE // 2 :]
                br, bi = b[:, : SIZE // 2], b[:, SIZE // 2 :]
                real = real + (ar * br + ai * bi)
                imag = imag + (ai * br - ar * bi)
            rank_one[p] = nyquist[first] * nyquist[second]
            return jnp.concatenate([real, imag], axis=1)

        def two(n, carry):
            both = jnp.concatenate([one(2 * n), one(2 * n + 1)], axis=0)
            cross[pl.ds(pl.multiple_of(n * 16, 16), 16), :] = both.astype(jnp.bfloat16)
            return carry

        lax.fori_loop(0, PAIRS // 2, two, 0)
        lagged = jnp.dot(cross[...], back_ref[...], preferred_element_type=jnp.float32)
        lagged = lagged.reshape(PAIRS, 8, LAGS)
        lagged = lagged + swap_halves(lagged)
        odd = lax.rem(lax.broadcasted_iota(jnp.int32, (PAIRS, 8, 128), 2), 2)
        weight = math.sqrt(WIN) / (2 * WIN)
        term = rank_one[...] * jnp.where(odd == 0, weight, -weight)
        lagged = lagged - jnp.concatenate([term, term], axis=2)
        slot = lax.broadcasted_iota(jnp.int32, lagged.shape, 0)
        lagged = jnp.where(slot < count_ref[0], lagged, 0.0)
        out_ref[:, c] = lagged[:, :4]

    def issue(n):
        if n % 2 == 0:
            raw_copies[n // 2].wait()
            lay_out(n // 2)
        if n == 0:
            pl.semaphore_wait(barrier, ST - 1 + 3)
        own_copy(n).start()
        for by in ORDER:
            y_copy(n, by).start()

    def forward(n):
        own_copy(n).wait()
        z_copy(n, 0).start()
        for by in ARRIVAL:
            y_copy(n, by).wait_recv()
            z_copy(n, by).start()

    def share(n):
        for by in (0, *ARRIVAL):
            z_copy(n, by).wait_recv()
            sibling_copy(n, by).start()

    def gather(n):
        for by in range(ST):
            sibling_copy(n, by).wait_recv()

    def compute_own(c):
        measure(c, 0)
        transform_first(c)
        transform_second(c, 0)

    def compute_rest(c):
        gather(2 * c)
        gather(2 * c + 1)
        for block in (2, 1):
            measure(c, block)
            transform_second(c, block)
        correlate(c)

    for n in range(WINDOW):
        issue(n)
    for copy in table_copies:
        copy.wait()
    row = lax.broadcasted_iota(jnp.int32, adder.shape, 0)
    column = lax.broadcasted_iota(jnp.int32, adder.shape, 1)
    sign = 1.0 - 2.0 * lax.rem(row, 2).astype(jnp.float32)
    weight = jnp.where(row < 256, jnp.where(column < 128, 1.0, 0.0), jnp.where(column < 128, 0.0, sign))
    adder[...] = weight.astype(jnp.bfloat16)
    for n in range(PIECES):
        forward(n)
        if n + WINDOW < PIECES:
            issue(n + WINDOW)
        if n:
            share(n - 1)
        if n % 2 == 0 and n:
            compute_rest(n // 2 - 1)
        if n % 2:
            compute_own(n // 2)
    share(PIECES - 1)
    compute_rest(COMP - 1)

    for n in range(PIECES):
        for by in range(ST):
            if by:
                y_copy(n, by).wait_send()
            z_copy(n, by).wait_send()
            sibling_copy(n, by).wait_send()


def shards(waveforms, pair_list, pair_count):
    forward, back = tables()
    windows = jnp.transpose(waveforms, (0, 2, 1, 3))
    slots = jnp.transpose(pair_list, (2, 0, 1))
    whole = pl.BlockSpec(memory_space=pltpu.VMEM)
    scalar = pl.BlockSpec(memory_space=pltpu.SMEM)
    anywhere = pl.BlockSpec(memory_space=pl.ANY)
    dma = pltpu.SemaphoreType.DMA
    result = pl.pallas_call(
        kernel,
        out_shape=jax.ShapeDtypeStruct((PAIRS, COMP, STATIONS, LAGS), jnp.float32),
        in_specs=[scalar, scalar, anywhere, anywhere, anywhere],
        out_specs=whole,
        scratch_shapes=[
            pltpu.VMEM((SIZE, SIZE), jnp.bfloat16),
            pltpu.VMEM((SIZE, LAGS), jnp.bfloat16),
            pltpu.VMEM((OWN, COMP, ST * STATIONS, WIN), jnp.bfloat16),
            pltpu.VMEM((COMP, ST, PART, HALF), jnp.bfloat16),
            pltpu.VMEM((3, COMP, ROWS, HALF), jnp.bfloat16),
            pltpu.VMEM((ROWS, HALF + 256), jnp.bfloat16),
            pltpu.VMEM((EVENTS, STEPS, 8, SIZE), jnp.float32),
            pltpu.VMEM((3 * EVENTS, STEPS, 8, SIZE), jnp.float32),
            pltpu.VMEM((3 * EVENTS, 8, 128), jnp.float32),
            pltpu.VMEM((3, EVENTS, 8, 128), jnp.float32),
            pltpu.VMEM((512, 256), jnp.bfloat16),
            pltpu.VMEM((PAIRS * 8, SIZE), jnp.bfloat16),
            pltpu.VMEM((PAIRS, 8, 128), jnp.float32),
            dma((2,)),
            dma((COMP,)),
            dma((PIECES,)),
            dma((PIECES, ST)),
            dma((PIECES, ST)),
            dma((PIECES, ST)),
            dma((PIECES, ST)),
            dma((PIECES, ST)),
            dma((PIECES, ST)),
        ],
        compiler_params=pltpu.CompilerParams(
            collective_id=0, has_side_effects=True, vmem_limit_bytes=58 * 2**20
        ),
        name="pair_correlation",
    )(slots, pair_count, windows, forward, back)
    return jnp.transpose(result, (0, 2, 1, 3))


def solution(mesh):
    in_specs = (P(("ev", "st"), None, None, None), P("ev", None, None), P("ev"))
    out_specs = P("ev", "st", None, None)
    return jax.shard_map(shards, mesh=mesh, in_specs=in_specs, out_specs=out_specs, check_vma=False)
```

```python
import math

import jax
import jax.numpy as jnp
import numpy as np
from jax import lax
from jax.experimental import pallas as pl
from jax.experimental.pallas import tpu as pltpu
from jax.sharding import PartitionSpec as P

MESH = pl.DeviceIdType.MESH
EV, ST = 64, 8
EVENTS, OWN, STATIONS, COMP, WIN = 32, 4, 4, 3, 2048
PAIRS, LAGS = 64, 256
HALF, CHUNK, SIZE = 1024, 256, 512
STEPS = HALF // CHUNK
ROWS = EVENTS * 8
PART = OWN * 8
PIECES = 2 * COMP
COLUMN = 8
TOGETHER = 4
ORDER = (4, 3, 5, 2, 6, 1, 7)


def tables():
    sample = np.arange(SIZE)[:, None]
    odd = 2 * np.arange(SIZE // 2)[None, :] + 1
    angle = (sample * odd % (2 * SIZE)) * (math.pi / SIZE)
    forward = np.concatenate([np.cos(angle), -np.sin(angle)], axis=1)
    weight = 2.0 / SIZE * math.sqrt(WIN)
    back = weight * forward[:LAGS].T
    return jnp.asarray(forward, jnp.bfloat16), jnp.asarray(back, jnp.bfloat16)


def upper(shape, axis):
    return lax.broadcasted_iota(jnp.int32, shape, axis) < 4


def swap_halves(value):
    return pltpu.roll(value, 4, 1)


def kernel(
    slots_ref, count_ref, wave_ref, forward_hbm, back_hbm, out_ref,
    forward_ref, back_ref, raw, parts, held, wide, first_spec, second_spec, nyquist, scales, adder, cross, rank_one,
    joined, table_sem, raw_sem, own_sem, y_send, y_recv, z_send, z_recv, s_send, s_recv,
):
    ev = lax.axis_index("ev")
    st = lax.axis_index("st")
    core = lax.rem(ev, 2)
    earlier = lax.rem(ev + EV - 2, EV)
    later = lax.rem(ev + 2, EV)
    sibling = ev + 1 - 2 * core

    raw_copies = []
    for c in range(COMP):
        copy = pltpu.make_async_copy(wave_ref.at[:, c], raw.at[:, c], raw_sem.at[c])
        copy.start()
        raw_copies.append(copy)
    table_copies = [
        pltpu.make_async_copy(forward_hbm, forward_ref, table_sem.at[0]),
        pltpu.make_async_copy(back_hbm, back_ref, table_sem.at[1]),
    ]
    for copy in table_copies:
        copy.start()

    barrier = pltpu.get_barrier_semaphore()
    first = lax.rem(ev // 2, COLUMN) == 0
    last = lax.rem(ev // 2, COLUMN) == COLUMN - 1
    for by in range(1, ST):
        pl.semaphore_signal(
            barrier, inc=1, device_id=(ev, lax.rem(st + by, ST)), device_id_type=MESH
        )
    pl.semaphore_signal(barrier, inc=1, device_id=(sibling, st), device_id_type=MESH)

    @pl.when(first)
    def _():
        pl.semaphore_signal(barrier, inc=1, device_id=(earlier, st), device_id_type=MESH)

    @pl.when(jnp.logical_not(last))
    def _():
        pl.semaphore_signal(barrier, inc=1, device_id=(later, st), device_id_type=MESH)

    def meet():
        before = jnp.where(first, 0, 1) + jnp.where(last, 1, 0)
        pl.semaphore_wait(barrier, ST + before)

        @pl.when(last)
        def _():
            pl.semaphore_signal(joined, inc=1, device_id=(later, st), device_id_type=MESH)

    def place(n, source):
        half = n % 2 * 16
        return n // 2, pl.ds(pl.multiple_of(source * PART + half, 16), 16), slice(half, half + 16)

    def y_copy(n, by):
        target = lax.rem(st + by, ST)
        c, rows, half = place(n, st)
        return pltpu.make_async_remote_copy(
            src_ref=parts.at[c, target, half],
            dst_ref=held.at[0, c, rows],
            send_sem=y_send.at[n, by],
            recv_sem=y_recv.at[n, by],
            device_id=(ev, target),
            device_id_type=MESH,
        )

    def own_copy(n):
        c, rows, half = place(n, st)
        return pltpu.make_async_copy(parts.at[c, st, half], held.at[0, c, rows], own_sem.at[n])

    def z_copy(n, by):
        c, rows, _ = place(n, lax.rem(st + ST - by, ST))
        return pltpu.make_async_remote_copy(
            src_ref=held.at[0, c, rows],
            dst_ref=held.at[2, c, rows],
            send_sem=z_send.at[n, by],
            recv_sem=z_recv.at[n, by],
            device_id=(earlier, st),
            device_id_type=MESH,
        )

    def sibling_copy(n, by):
        c, rows, _ = place(n, lax.rem(st + ST - by, ST))
        return pltpu.make_async_remote_copy(
            src_ref=held.at[2 - 2 * core, c, rows],
            dst_ref=held.at[1, c, rows],
            send_sem=s_send.at[n, by],
            recv_sem=s_recv.at[n, by],
            device_id=(sibling, st),
            device_id_type=MESH,
        )

    def lay_out(c):
        def group(g, carry):
            stations = pl.ds(pl.multiple_of(g * 16, 16), 16)
            for pair in range(OWN // 2):
                for piece in range(HALF // 256):
                    low = slice(piece * 256, piece * 256 + 256)
                    high = slice(HALF + piece * 256, HALF + piece * 256 + 256)
                    made = [[], [], [], []]
                    for e in (2 * pair, 2 * pair + 1):
                        head = raw[e, c, stations, low].astype(jnp.float32)
                        tail = raw[e, c, stations, high].astype(jnp.float32)
                        for t in range(2):
                            h0 = head[8 * t : 8 * t + 8]
                            h1 = tail[8 * t : 8 * t + 8]
                            top = upper(h0.shape, 0)
                            made[2 * t].append(jnp.where(top, h0, pltpu.roll(h1, 4, 0)))
                            made[2 * t + 1].append(jnp.where(top, pltpu.roll(h0, 4, 0), h1))
                    for d in range(4):
                        both = jnp.concatenate(made[d], axis=0).astype(jnp.bfloat16)
                        parts[c, 4 * g + d, 16 * pair : 16 * pair + 16, low] = both
            return carry

        lax.fori_loop(0, 2, group, 0)

    def half_of(c, half, block, lanes):
        rows = [held[block, c, PART * k + 16 * half : PART * k + 16 * half + 16, lanes] for k in range(ST)]
        return jnp.concatenate(rows, axis=0)

    def events_of(half, block):
        return [pl.ds(block * EVENTS + OWN * k + 2 * half, 2) for k in range(ST)]

    def measure(c, half, block):
        energy = jnp.zeros((ROWS // 2, 128), jnp.float32)
        total = jnp.zeros((ROWS // 2, 128), jnp.float32)
        for piece in range(HALF // 128):
            x = half_of(c, half, block, slice(128 * piece, 128 * piece + 128)).astype(jnp.float32)
            energy = energy + x * x
            total = total + x
        split = []
        for value in (energy, total):
            high = value.astype(jnp.bfloat16)
            wide_high = high.astype(jnp.float32)
            rest = jnp.where(jnp.abs(wide_high) < jnp.inf, value - wide_high, 0.0)
            split += [high, rest.astype(jnp.bfloat16)]
        sums = jnp.dot(
            jnp.concatenate(split, axis=1), adder[...], preferred_element_type=jnp.float32
        ).reshape(EVENTS // 2, 8, 256)
        sums = sums + swap_halves(sums)
        scale = 1.0 / jnp.sqrt(WIN * (sums[:, :, :128] * (1.0 / WIN) + 1e-6))
        alternate = sums[:, :, 128:] * scale
        for k, events in enumerate(events_of(half, block)):
            scales[events] = scale[2 * k : 2 * k + 2]
            nyquist[events] = alternate[2 * k : 2 * k + 2]
        return scale

    def scaled(product, scale):
        product = product.reshape(scale.shape[0], 8, SIZE)
        return jnp.concatenate(
            [product[:, :, 128 * n : 128 * n + 128] * scale for n in range(SIZE // 128)], axis=2
        )

    def transform_first(c):
        x = held[0, c]
        head = swap_halves(x[:, :128].astype(jnp.float32).reshape(EVENTS, 8, 128))
        tail = swap_halves(x[:, HALF - 128 :].astype(jnp.float32).reshape(EVENTS, 8, 128))
        top = upper(head.shape, 1)
        before = jnp.where(top, 0.0, tail).reshape(ROWS, 128).astype(jnp.bfloat16)
        after = jnp.where(top, head, 0.0).reshape(ROWS, 128).astype(jnp.bfloat16)
        wide[:, :128] = before
        wide[:, 128 : 128 + HALF] = x
        wide[:, 128 + HALF :] = after
        for q in range(STEPS):
            product = jnp.dot(
                wide[:, CHUNK * q : CHUNK * q + SIZE],
                forward_ref[...],
                preferred_element_type=jnp.float32,
            )
            first_spec[:, q] = scaled(product, scales[:EVENTS])

    def transform_second(c, half, block):
        scale = measure(c, half, block)
        for q in range(STEPS):
            product = jnp.dot(
                half_of(c, half, block, slice(CHUNK * q, CHUNK * q + CHUNK)),
                forward_ref[:CHUNK, :],
                preferred_element_type=jnp.float32,
            )
            product = scaled(product, scale)
            for k, events in enumerate(events_of(half, block)):
                second_spec[events, q] = product[2 * k : 2 * k + 2]

    def correlate(c):
        def one(p):
            first = slots_ref[0, 0, p]
            second = slots_ref[1, 0, p] * EVENTS + slots_ref[2, 0, p]
            real = jnp.zeros((8, SIZE // 2), jnp.float32)
            imag = jnp.zeros((8, SIZE // 2), jnp.float32)
            for q in range(STEPS):
                a = first_spec[first, q]
                b = second_spec[second, q]
                ar, ai = a[:, : SIZE // 2], a[:, SIZE // 2 :]
                br, bi = b[:, : SIZE // 2], b[:, SIZE // 2 :]
                real = real + (ar * br + ai * bi)
                imag = imag + (ai * br - ar * bi)
            rank_one[p] = nyquist[first] * nyquist[second]
            return jnp.concatenate([real, imag], axis=1)

        def some(n, carry):
            made = jnp.concatenate([one(TOGETHER * n + k) for k in range(TOGETHER)], axis=0)
            rows = pl.ds(pl.multiple_of(n * 8 * TOGETHER, 8 * TOGETHER), 8 * TOGETHER)
            cross[rows, :] = made.astype(jnp.bfloat16)
            return carry

        lax.fori_loop(0, PAIRS // TOGETHER, some, 0)
        lagged = jnp.dot(cross[...], back_ref[...], preferred_element_type=jnp.float32)
        lagged = lagged.reshape(PAIRS, 8, LAGS)
        lagged = lagged + swap_halves(lagged)
        odd = lax.rem(lax.broadcasted_iota(jnp.int32, (PAIRS, 8, 128), 2), 2)
        weight = math.sqrt(WIN) / (2 * WIN)
        term = rank_one[...] * jnp.where(odd == 0, weight, -weight)
        lagged = lagged - jnp.concatenate([term, term], axis=2)
        slot = lax.broadcasted_iota(jnp.int32, lagged.shape, 0)
        lagged = jnp.where(slot < count_ref[0], lagged, 0.0)
        out_ref[:, c] = lagged[:, :4]

    def issue(n):
        if n % 2 == 0:
            raw_copies[n // 2].wait()
            lay_out(n // 2)
        if n == 0:
            meet()
        own_copy(n).start()
        for by in ORDER:
            y_copy(n, by).start()

    def forward(n):
        for by in ORDER:
            y_copy(n, by).wait_recv()
            z_copy(n, by).start()

    def share(n):
        for by in (0, *ORDER):
            z_copy(n, by).wait_recv()
            sibling_copy(n, by).start()

    def gather(n):
        for by in range(ST):
            sibling_copy(n, by).wait_recv()

    def compute_own(n):
        transform_second(n // 2, n % 2, 0)
        if n % 2:
            transform_first(n // 2)

    def compute_rest(n):
        share(n)
        transform_second(n // 2, n % 2, 2)
        gather(n)
        transform_second(n // 2, n % 2, 1)
        if n % 2:
            correlate(n // 2)

    for n in range(PIECES):
        issue(n)

    @pl.when(first)
    def _():
        pl.semaphore_wait(joined, 1)

    for n in range(PIECES):
        own_copy(n).wait()
        z_copy(n, 0).start()
    for copy in table_copies:
        copy.wait()
    row = lax.broadcasted_iota(jnp.int32, adder.shape, 0)
    column = lax.broadcasted_iota(jnp.int32, adder.shape, 1)
    sign = 1.0 - 2.0 * lax.rem(row, 2).astype(jnp.float32)
    weight = jnp.where(row < 256, jnp.where(column < 128, 1.0, 0.0), jnp.where(column < 128, 0.0, sign))
    adder[...] = weight.astype(jnp.bfloat16)
    for n in range(PIECES):
        forward(n)
        if n:
            compute_rest(n - 1)
        compute_own(n)
    compute_rest(PIECES - 1)

    for n in range(PIECES):
        for by in range(ST):
            if by:
                y_copy(n, by).wait_send()
            z_copy(n, by).wait_send()
            sibling_copy(n, by).wait_send()


def shards(waveforms, pair_list, pair_count):
    forward, back = tables()
    windows = jnp.transpose(waveforms, (0, 2, 1, 3))
    slots = jnp.transpose(pair_list, (2, 0, 1))
    whole = pl.BlockSpec(memory_space=pltpu.VMEM)
    scalar = pl.BlockSpec(memory_space=pltpu.SMEM)
    anywhere = pl.BlockSpec(memory_space=pl.ANY)
    dma = pltpu.SemaphoreType.DMA
    result = pl.pallas_call(
        kernel,
        out_shape=jax.ShapeDtypeStruct((PAIRS, COMP, STATIONS, LAGS), jnp.float32),
        in_specs=[scalar, scalar, anywhere, anywhere, anywhere],
        out_specs=whole,
        scratch_shapes=[
            pltpu.VMEM((SIZE, SIZE), jnp.bfloat16),
            pltpu.VMEM((SIZE, LAGS), jnp.bfloat16),
            pltpu.VMEM((OWN, COMP, ST * STATIONS, WIN), jnp.bfloat16),
            pltpu.VMEM((COMP, ST, PART, HALF), jnp.bfloat16),
            pltpu.VMEM((3, COMP, ROWS, HALF), jnp.bfloat16),
            pltpu.VMEM((ROWS, HALF + 256), jnp.bfloat16),
            pltpu.VMEM((EVENTS, STEPS, 8, SIZE), jnp.float32),
            pltpu.VMEM((3 * EVENTS, STEPS, 8, SIZE), jnp.float32),
            pltpu.VMEM((3 * EVENTS, 8, 128), jnp.float32),
            pltpu.VMEM((3 * EVENTS, 8, 128), jnp.float32),
            pltpu.VMEM((512, 256), jnp.bfloat16),
            pltpu.VMEM((PAIRS * 8, SIZE), jnp.bfloat16),
            pltpu.VMEM((PAIRS, 8, 128), jnp.float32),
            pltpu.SemaphoreType.REGULAR,
            dma((2,)),
            dma((COMP,)),
            dma((PIECES,)),
            dma((PIECES, ST)),
            dma((PIECES, ST)),
            dma((PIECES, ST)),
            dma((PIECES, ST)),
            dma((PIECES, ST)),
            dma((PIECES, ST)),
        ],
        compiler_params=pltpu.CompilerParams(
            collective_id=0, has_side_effects=True, vmem_limit_bytes=58 * 2**20
        ),
        name="pair_correlation",
    )(slots, pair_count, windows, forward, back)
    return jnp.transpose(result, (0, 2, 1, 3))


def solution(mesh):
    in_specs = (P(("ev", "st"), None, None, None), P("ev", None, None), P("ev"))
    out_specs = P("ev", "st", None, None)
    return jax.shard_map(shards, mesh=mesh, in_specs=in_specs, out_specs=out_specs, check_vma=False)
```

```python
import math

import jax
import jax.numpy as jnp
import numpy as np
from jax import lax
from jax.experimental import pallas as pl
from jax.experimental.pallas import tpu as pltpu
from jax.sharding import PartitionSpec as P

MESH = pl.DeviceIdType.MESH
EV, ST = 64, 8
EVENTS, OWN, STATIONS, COMP, WIN = 32, 4, 4, 3, 2048
PAIRS, LAGS = 64, 256
HALF, CHUNK, SIZE = 1024, 256, 512
STEPS = HALF // CHUNK
ROWS = EVENTS * 8
PIECES = 2 * COMP
COLUMN = 8
TOGETHER = 4
ORDER = (4, 3, 5, 2, 6, 1, 7)


def tables():
    sample = np.arange(SIZE)[:, None]
    odd = 2 * np.arange(SIZE // 2)[None, :] + 1
    angle = (sample * odd % (2 * SIZE)) * (math.pi / SIZE)
    forward = np.concatenate([np.cos(angle), -np.sin(angle)], axis=1)
    weight = 2.0 / SIZE * math.sqrt(WIN)
    back = weight * forward[:LAGS].T
    return jnp.asarray(forward, jnp.bfloat16), jnp.asarray(back, jnp.bfloat16)


def upper(shape, axis):
    return lax.broadcasted_iota(jnp.int32, shape, axis) < 4


def swap_halves(value):
    return pltpu.roll(value, 4, 1)


def kernel(
    slots_ref, count_ref, wave_ref, forward_hbm, back_hbm, out_ref,
    forward_ref, back_ref, raw, parts, held, wide, first_spec, second_spec, nyquist, adder, cross, rank_one,
    joined, table_sem, raw_sem, own_sem, y_send, y_recv, z_send, z_recv, s_send, s_recv,
):
    ev = lax.axis_index("ev")
    st = lax.axis_index("st")
    core = lax.rem(ev, 2)
    earlier = lax.rem(ev + EV - 2, EV)
    later = lax.rem(ev + 2, EV)
    sibling = ev + 1 - 2 * core

    raw_copies = []
    for c in range(COMP):
        copy = pltpu.make_async_copy(wave_ref.at[:, c], raw.at[:, c], raw_sem.at[c])
        copy.start()
        raw_copies.append(copy)
    table_copies = [
        pltpu.make_async_copy(forward_hbm, forward_ref, table_sem.at[0]),
        pltpu.make_async_copy(back_hbm, back_ref, table_sem.at[1]),
    ]
    for copy in table_copies:
        copy.start()

    barrier = pltpu.get_barrier_semaphore()
    first = lax.rem(ev // 2, COLUMN) == 0
    last = lax.rem(ev // 2, COLUMN) == COLUMN - 1
    for by in range(1, ST):
        pl.semaphore_signal(
            barrier, inc=1, device_id=(ev, lax.rem(st + by, ST)), device_id_type=MESH
        )
    pl.semaphore_signal(barrier, inc=1, device_id=(sibling, st), device_id_type=MESH)

    @pl.when(first)
    def _():
        pl.semaphore_signal(barrier, inc=1, device_id=(earlier, st), device_id_type=MESH)

    @pl.when(jnp.logical_not(last))
    def _():
        pl.semaphore_signal(barrier, inc=1, device_id=(later, st), device_id_type=MESH)

    def meet():
        before = jnp.where(first, 0, 1) + jnp.where(last, 1, 0)
        pl.semaphore_wait(barrier, ST + before)

        @pl.when(last)
        def _():
            pl.semaphore_signal(joined, inc=1, device_id=(later, st), device_id_type=MESH)

    def rows_of(source):
        return pl.ds(pl.multiple_of(source * 16, 16), 16)

    def y_copy(n, by):
        c, half = n // 2, n % 2
        target = lax.rem(st + by, ST)
        return pltpu.make_async_remote_copy(
            src_ref=parts.at[c, target, half],
            dst_ref=held.at[0, c, half, rows_of(st)],
            send_sem=y_send.at[n],
            recv_sem=y_recv.at[n, by],
            device_id=(ev, target),
            device_id_type=MESH,
        )

    def own_copy(n):
        c, half = n // 2, n % 2
        return pltpu.make_async_copy(
            parts.at[c, st, half], held.at[0, c, half, rows_of(st)], own_sem.at[n]
        )

    def z_copy(n, rows):
        c, half = n // 2, n % 2
        return pltpu.make_async_remote_copy(
            src_ref=held.at[0, c, half, rows],
            dst_ref=held.at[2, c, half, rows],
            send_sem=z_send.at[n],
            recv_sem=z_recv.at[n],
            device_id=(earlier, st),
            device_id_type=MESH,
        )

    def sibling_copy(n):
        c, half = n // 2, n % 2
        return pltpu.make_async_remote_copy(
            src_ref=held.at[2 - 2 * core, c, half],
            dst_ref=held.at[1, c, half],
            send_sem=s_send.at[n],
            recv_sem=s_recv.at[n],
            device_id=(sibling, st),
            device_id_type=MESH,
        )

    every = pl.ds(0, 16 * ST)

    def y_sent(n):
        rows = pl.ds(0, 16 * (ST - 1))
        return pltpu.make_async_remote_copy(
            src_ref=held.at[0, n // 2, n % 2, rows],
            dst_ref=held.at[0, n // 2, n % 2, rows],
            send_sem=y_send.at[n],
            recv_sem=y_recv.at[n, 0],
            device_id=(ev, lax.rem(st + 1, ST)),
            device_id_type=MESH,
        )

    def lay_out(c):
        def group(g, carry):
            stations = pl.ds(pl.multiple_of(g * 16, 16), 16)
            for pair in range(OWN // 2):
                for piece in range(HALF // 256):
                    low = slice(piece * 256, piece * 256 + 256)
                    high = slice(HALF + piece * 256, HALF + piece * 256 + 256)
                    made = [[], [], [], []]
                    for e in (2 * pair, 2 * pair + 1):
                        head = raw[e, c, stations, low].astype(jnp.float32)
                        tail = raw[e, c, stations, high].astype(jnp.float32)
                        for t in range(2):
                            h0 = head[8 * t : 8 * t + 8]
                            h1 = tail[8 * t : 8 * t + 8]
                            top = upper(h0.shape, 0)
                            made[2 * t].append(jnp.where(top, h0, pltpu.roll(h1, 4, 0)))
                            made[2 * t + 1].append(jnp.where(top, pltpu.roll(h0, 4, 0), h1))
                    for d in range(4):
                        both = jnp.concatenate(made[d], axis=0).astype(jnp.bfloat16)
                        parts[c, 4 * g + d, pair, :, low] = both
            return carry

        lax.fori_loop(0, 2, group, 0)

    def events_of(half, block):
        return [pl.ds(block * EVENTS + OWN * k + 2 * half, 2) for k in range(ST)]

    def measure(c, half, block):
        energy = jnp.zeros((ROWS // 2, 128), jnp.float32)
        total = jnp.zeros((ROWS // 2, 128), jnp.float32)
        for piece in range(HALF // 128):
            x = held[block, c, half, :, 128 * piece : 128 * piece + 128].astype(jnp.float32)
            energy = energy + x * x
            total = total + x
        split = []
        for value in (energy, total):
            high = value.astype(jnp.bfloat16)
            wide_high = high.astype(jnp.float32)
            rest = jnp.where(jnp.abs(wide_high) < jnp.inf, value - wide_high, 0.0)
            split += [high, rest.astype(jnp.bfloat16)]
        sums = jnp.dot(
            jnp.concatenate(split, axis=1), adder[...], preferred_element_type=jnp.float32
        ).reshape(EVENTS // 2, 8, 256)
        sums = sums + swap_halves(sums)
        scale = 1.0 / jnp.sqrt(WIN * (sums[:, :, :128] * (1.0 / WIN) + 1e-6))
        alternate = sums[:, :, 128:] * scale
        for k, events in enumerate(events_of(half, block)):
            nyquist[events] = alternate[2 * k : 2 * k + 2]
        return scale

    def scaled(product, scale):
        product = product.reshape(scale.shape[0], 8, SIZE)
        return jnp.concatenate(
            [product[:, :, 128 * n : 128 * n + 128] * scale for n in range(SIZE // 128)], axis=2
        )

    def transform_first(c, half, scale):
        x = held[0, c, half]
        head = swap_halves(x[:, :128].astype(jnp.float32).reshape(EVENTS // 2, 8, 128))
        tail = swap_halves(x[:, HALF - 128 :].astype(jnp.float32).reshape(EVENTS // 2, 8, 128))
        top = upper(head.shape, 1)
        before = jnp.where(top, 0.0, tail).reshape(ROWS // 2, 128).astype(jnp.bfloat16)
        after = jnp.where(top, head, 0.0).reshape(ROWS // 2, 128).astype(jnp.bfloat16)
        wide[:, :128] = before
        wide[:, 128 : 128 + HALF] = x
        wide[:, 128 + HALF :] = after
        for q in range(STEPS):
            product = jnp.dot(
                wide[:, CHUNK * q : CHUNK * q + SIZE],
                forward_ref[...],
                preferred_element_type=jnp.float32,
            )
            product = scaled(product, scale)
            for k, events in enumerate(events_of(half, 0)):
                first_spec[events, q] = product[2 * k : 2 * k + 2]

    def transform_second(c, half, block):
        scale = measure(c, half, block)
        for q in range(STEPS):
            product = jnp.dot(
                held[block, c, half, :, CHUNK * q : CHUNK * q + CHUNK],
                forward_ref[:CHUNK, :],
                preferred_element_type=jnp.float32,
            )
            product = scaled(product, scale)
            for k, events in enumerate(events_of(half, block)):
                second_spec[events, q] = product[2 * k : 2 * k + 2]
        return scale

    def correlate(c):
        def one(p):
            first = slots_ref[0, 0, p]
            second = slots_ref[1, 0, p] * EVENTS + slots_ref[2, 0, p]
            real = jnp.zeros((8, SIZE // 2), jnp.float32)
            imag = jnp.zeros((8, SIZE // 2), jnp.float32)
            for q in range(STEPS):
                a = first_spec[first, q]
                b = second_spec[second, q]
                ar, ai = a[:, : SIZE // 2], a[:, SIZE // 2 :]
                br, bi = b[:, : SIZE // 2], b[:, SIZE // 2 :]
                real = real + (ar * br + ai * bi)
                imag = imag + (ai * br - ar * bi)
            rank_one[p] = nyquist[first] * nyquist[second]
            return jnp.concatenate([real, imag], axis=1)

        def some(n, carry):
            made = jnp.concatenate([one(TOGETHER * n + k) for k in range(TOGETHER)], axis=0)
            rows = pl.ds(pl.multiple_of(n * 8 * TOGETHER, 8 * TOGETHER), 8 * TOGETHER)
            cross[rows, :] = made.astype(jnp.bfloat16)
            return carry

        lax.fori_loop(0, PAIRS // TOGETHER, some, 0)
        lagged = jnp.dot(cross[...], back_ref[...], preferred_element_type=jnp.float32)
        lagged = lagged.reshape(PAIRS, 8, LAGS)
        lagged = lagged + swap_halves(lagged)
        odd = lax.rem(lax.broadcasted_iota(jnp.int32, (PAIRS, 8, 128), 2), 2)
        weight = math.sqrt(WIN) / (2 * WIN)
        term = rank_one[...] * jnp.where(odd == 0, weight, -weight)
        lagged = lagged - jnp.concatenate([term, term], axis=2)
        slot = lax.broadcasted_iota(jnp.int32, lagged.shape, 0)
        lagged = jnp.where(slot < count_ref[0], lagged, 0.0)
        out_ref[:, c] = lagged[:, :4]

    def issue(n):
        if n % 2 == 0:
            raw_copies[n // 2].wait()
            lay_out(n // 2)
        if n == 0:
            meet()
        own_copy(n).start()
        for by in ORDER:
            y_copy(n, by).start()

    def forward(n):
        for by in ORDER:
            y_copy(n, by).wait_recv()
            z_copy(n, rows_of(lax.rem(st + ST - by, ST))).start()

    def compute_own(n):
        scale = transform_second(n // 2, n % 2, 0)
        transform_first(n // 2, n % 2, scale)

    def compute_rest(n):
        z_copy(n, every).wait_recv()
        sibling_copy(n).start()
        transform_second(n // 2, n % 2, 2)
        sibling_copy(n).wait_recv()
        transform_second(n // 2, n % 2, 1)
        if n % 2:
            correlate(n // 2)

    for n in range(PIECES):
        issue(n)

    @pl.when(first)
    def _():
        pl.semaphore_wait(joined, 1)

    for n in range(PIECES):
        own_copy(n).wait()
        z_copy(n, rows_of(st)).start()
    for copy in table_copies:
        copy.wait()
    row = lax.broadcasted_iota(jnp.int32, adder.shape, 0)
    column = lax.broadcasted_iota(jnp.int32, adder.shape, 1)
    sign = 1.0 - 2.0 * lax.rem(row, 2).astype(jnp.float32)
    weight = jnp.where(row < 256, jnp.where(column < 128, 1.0, 0.0), jnp.where(column < 128, 0.0, sign))
    adder[...] = weight.astype(jnp.bfloat16)
    for n in range(PIECES):
        forward(n)
        if n:
            compute_rest(n - 1)
        compute_own(n)
    compute_rest(PIECES - 1)

    for n in range(PIECES):
        y_sent(n).wait_send()
        z_copy(n, every).wait_send()
        sibling_copy(n).wait_send()


def shards(waveforms, pair_list, pair_count):
    forward, back = tables()
    windows = jnp.transpose(waveforms, (0, 2, 1, 3))
    slots = jnp.transpose(pair_list, (2, 0, 1))
    whole = pl.BlockSpec(memory_space=pltpu.VMEM)
    scalar = pl.BlockSpec(memory_space=pltpu.SMEM)
    anywhere = pl.BlockSpec(memory_space=pl.ANY)
    dma = pltpu.SemaphoreType.DMA
    result = pl.pallas_call(
        kernel,
        out_shape=jax.ShapeDtypeStruct((PAIRS, COMP, STATIONS, LAGS), jnp.float32),
        in_specs=[scalar, scalar, anywhere, anywhere, anywhere],
        out_specs=whole,
        scratch_shapes=[
            pltpu.VMEM((SIZE, SIZE), jnp.bfloat16),
            pltpu.VMEM((SIZE, LAGS), jnp.bfloat16),
            pltpu.VMEM((OWN, COMP, ST * STATIONS, WIN), jnp.bfloat16),
            pltpu.VMEM((COMP, ST, 2, 16, HALF), jnp.bfloat16),
            pltpu.VMEM((3, COMP, 2, 16 * ST, HALF), jnp.bfloat16),
            pltpu.VMEM((ROWS // 2, HALF + 256), jnp.bfloat16),
            pltpu.VMEM((EVENTS, STEPS, 8, SIZE), jnp.float32),
            pltpu.VMEM((3 * EVENTS, STEPS, 8, SIZE), jnp.float32),
            pltpu.VMEM((3 * EVENTS, 8, 128), jnp.float32),
            pltpu.VMEM((512, 256), jnp.bfloat16),
            pltpu.VMEM((PAIRS * 8, SIZE), jnp.bfloat16),
            pltpu.VMEM((PAIRS, 8, 128), jnp.float32),
            pltpu.SemaphoreType.REGULAR,
            dma((2,)),
            dma((COMP,)),
            dma((PIECES,)),
            dma((PIECES,)),
            dma((PIECES, ST)),
            dma((PIECES,)),
            dma((PIECES,)),
            dma((PIECES,)),
            dma((PIECES,)),
        ],
        compiler_params=pltpu.CompilerParams(
            collective_id=0, has_side_effects=True, vmem_limit_bytes=58 * 2**20
        ),
        name="pair_correlation",
    )(slots, pair_count, windows, forward, back)
    return jnp.transpose(result, (0, 2, 1, 3))


def solution(mesh):
    in_specs = (P(("ev", "st"), None, None, None), P("ev", None, None), P("ev"))
    out_specs = P("ev", "st", None, None)
    return jax.shard_map(shards, mesh=mesh, in_specs=in_specs, out_specs=out_specs, check_vma=False)
```

```python
import math

import jax
import jax.numpy as jnp
from jax import lax
from jax.experimental import pallas as pl
from jax.experimental.pallas import tpu as pltpu
from jax.sharding import PartitionSpec as P

MESH = pl.DeviceIdType.MESH
EV, ST = 64, 8
EVENTS, OWN, STATIONS, COMP, WIN = 32, 4, 4, 3, 2048
PAIRS, LAGS = 64, 256
HALF, CHUNK, SIZE = 1024, 256, 512
STEPS = HALF // CHUNK
ROWS = EVENTS * 8
PIECES = 2 * COMP
COLUMN = 8
TOGETHER = 4
ORDER = (4, 3, 5, 2, 6, 1, 7)


def upper(shape, axis):
    return lax.broadcasted_iota(jnp.int32, shape, axis) < 4


def swap_halves(value):
    return pltpu.roll(value, 4, 1)


def kernel(
    slots_ref, count_ref, wave_ref, out_ref,
    forward_ref, back_ref, raw, parts, held, wide, first_spec, second_spec, nyquist, adder, cross, rank_one,
    joined, raw_sem, own_sem, y_send, y_recv, z_send, z_recv, s_send, s_recv,
):
    ev = lax.axis_index("ev")
    st = lax.axis_index("st")
    core = lax.rem(ev, 2)
    earlier = lax.rem(ev + EV - 2, EV)
    later = lax.rem(ev + 2, EV)
    sibling = ev + 1 - 2 * core

    raw_copies = []
    for c in range(COMP):
        copy = pltpu.make_async_copy(wave_ref.at[:, c], raw.at[:, c], raw_sem.at[c])
        copy.start()
        raw_copies.append(copy)
    barrier = pltpu.get_barrier_semaphore()
    first = lax.rem(ev // 2, COLUMN) == 0
    last = lax.rem(ev // 2, COLUMN) == COLUMN - 1
    for by in range(1, ST):
        pl.semaphore_signal(
            barrier, inc=1, device_id=(ev, lax.rem(st + by, ST)), device_id_type=MESH
        )
    pl.semaphore_signal(barrier, inc=1, device_id=(sibling, st), device_id_type=MESH)

    @pl.when(first)
    def _():
        pl.semaphore_signal(barrier, inc=1, device_id=(earlier, st), device_id_type=MESH)

    @pl.when(jnp.logical_not(last))
    def _():
        pl.semaphore_signal(barrier, inc=1, device_id=(later, st), device_id_type=MESH)

    def meet():
        before = jnp.where(first, 0, 1) + jnp.where(last, 1, 0)
        pl.semaphore_wait(barrier, ST + before)

        @pl.when(last)
        def _():
            pl.semaphore_signal(joined, inc=1, device_id=(later, st), device_id_type=MESH)

    def rows_of(source):
        return pl.ds(pl.multiple_of(source * 16, 16), 16)

    def y_copy(n, by):
        c, half = n // 2, n % 2
        target = lax.rem(st + by, ST)
        return pltpu.make_async_remote_copy(
            src_ref=parts.at[c, target, half],
            dst_ref=held.at[0, c, half, rows_of(st)],
            send_sem=y_send.at[n],
            recv_sem=y_recv.at[n, by],
            device_id=(ev, target),
            device_id_type=MESH,
        )

    def own_copy(n):
        c, half = n // 2, n % 2
        return pltpu.make_async_copy(
            parts.at[c, st, half], held.at[0, c, half, rows_of(st)], own_sem.at[n]
        )

    def z_copy(n, rows):
        c, half = n // 2, n % 2
        return pltpu.make_async_remote_copy(
            src_ref=held.at[0, c, half, rows],
            dst_ref=held.at[2, c, half, rows],
            send_sem=z_send.at[n],
            recv_sem=z_recv.at[n],
            device_id=(earlier, st),
            device_id_type=MESH,
        )

    def sibling_copy(n):
        c, half = n // 2, n % 2
        return pltpu.make_async_remote_copy(
            src_ref=held.at[2 - 2 * core, c, half],
            dst_ref=held.at[1, c, half],
            send_sem=s_send.at[n],
            recv_sem=s_recv.at[n],
            device_id=(sibling, st),
            device_id_type=MESH,
        )

    every = pl.ds(0, 16 * ST)

    def y_sent(n):
        rows = pl.ds(0, 16 * (ST - 1))
        return pltpu.make_async_remote_copy(
            src_ref=held.at[0, n // 2, n % 2, rows],
            dst_ref=held.at[0, n // 2, n % 2, rows],
            send_sem=y_send.at[n],
            recv_sem=y_recv.at[n, 0],
            device_id=(ev, lax.rem(st + 1, ST)),
            device_id_type=MESH,
        )

    def make_tables():
        def turns(rows, step):
            shape = (rows, SIZE // 2)
            odd = 2 * lax.broadcasted_iota(jnp.int32, shape, 1) + 1
            phase = lax.rem(step * lax.broadcasted_iota(jnp.int32, shape, 0) * odd, 2 * SIZE)
            angle = phase.astype(jnp.float32) * (math.pi / SIZE)
            return jnp.cos(angle), jnp.sin(angle)

        fine_cos, fine_sin = turns(16, 1)
        coarse_cos, coarse_sin = turns(SIZE // 16, 16)
        halves = [[], []]
        for n in range(SIZE // 16):
            c, s = coarse_cos[n : n + 1], coarse_sin[n : n + 1]
            cosine = c * fine_cos - s * fine_sin
            sine = -(s * fine_cos + c * fine_sin)
            rows = slice(16 * n, 16 * n + 16)
            forward_ref[rows, : SIZE // 2] = cosine.astype(jnp.bfloat16)
            forward_ref[rows, SIZE // 2 :] = sine.astype(jnp.bfloat16)
            if n < LAGS // 16:
                halves[0].append(cosine)
                halves[1].append(sine)
        weight = 2.0 / SIZE * math.sqrt(WIN)
        for k, half in enumerate(halves):
            table = weight * jnp.transpose(jnp.concatenate(half, axis=0))
            back_ref[k * (SIZE // 2) : (k + 1) * (SIZE // 2), :] = table.astype(jnp.bfloat16)

    def lay_out(c):
        def group(g, carry):
            stations = pl.ds(pl.multiple_of(g * 16, 16), 16)
            for pair in range(OWN // 2):
                for piece in range(HALF // 256):
                    low = slice(piece * 256, piece * 256 + 256)
                    high = slice(HALF + piece * 256, HALF + piece * 256 + 256)
                    made = [[], [], [], []]
                    for e in (2 * pair, 2 * pair + 1):
                        head = raw[e, c, stations, low].astype(jnp.float32)
                        tail = raw[e, c, stations, high].astype(jnp.float32)
                        for t in range(2):
                            h0 = head[8 * t : 8 * t + 8]
                            h1 = tail[8 * t : 8 * t + 8]
                            top = upper(h0.shape, 0)
                            made[2 * t].append(jnp.where(top, h0, pltpu.roll(h1, 4, 0)))
                            made[2 * t + 1].append(jnp.where(top, pltpu.roll(h0, 4, 0), h1))
                    for d in range(4):
                        both = jnp.concatenate(made[d], axis=0).astype(jnp.bfloat16)
                        parts[c, 4 * g + d, pair, :, low] = both
            return carry

        lax.fori_loop(0, 2, group, 0)

    def events_of(half, block):
        return [pl.ds(block * EVENTS + OWN * k + 2 * half, 2) for k in range(ST)]

    def measure(c, half, block):
        energy = jnp.zeros((ROWS // 2, 128), jnp.float32)
        total = jnp.zeros((ROWS // 2, 128), jnp.float32)
        for piece in range(HALF // 128):
            x = held[block, c, half, :, 128 * piece : 128 * piece + 128].astype(jnp.float32)
            energy = energy + x * x
            total = total + x
        split = []
        for value in (energy, total):
            high = value.astype(jnp.bfloat16)
            wide_high = high.astype(jnp.float32)
            rest = jnp.where(jnp.abs(wide_high) < jnp.inf, value - wide_high, 0.0)
            split += [high, rest.astype(jnp.bfloat16)]
        sums = jnp.dot(
            jnp.concatenate(split, axis=1), adder[...], preferred_element_type=jnp.float32
        ).reshape(EVENTS // 2, 8, 256)
        sums = sums + swap_halves(sums)
        scale = 1.0 / jnp.sqrt(WIN * (sums[:, :, :128] * (1.0 / WIN) + 1e-6))
        alternate = sums[:, :, 128:] * scale
        for k, events in enumerate(events_of(half, block)):
            nyquist[events] = alternate[2 * k : 2 * k + 2]
        return scale

    def scaled(product, scale):
        product = product.reshape(scale.shape[0], 8, SIZE)
        return jnp.concatenate(
            [product[:, :, 128 * n : 128 * n + 128] * scale for n in range(SIZE // 128)], axis=2
        )

    def transform_first(c, half, scale):
        x = held[0, c, half]
        head = swap_halves(x[:, :128].astype(jnp.float32).reshape(EVENTS // 2, 8, 128))
        tail = swap_halves(x[:, HALF - 128 :].astype(jnp.float32).reshape(EVENTS // 2, 8, 128))
        top = upper(head.shape, 1)
        before = jnp.where(top, 0.0, tail).reshape(ROWS // 2, 128).astype(jnp.bfloat16)
        after = jnp.where(top, head, 0.0).reshape(ROWS // 2, 128).astype(jnp.bfloat16)
        wide[:, :128] = before
        wide[:, 128 : 128 + HALF] = x
        wide[:, 128 + HALF :] = after
        for q in range(STEPS):
            product = jnp.dot(
                wide[:, CHUNK * q : CHUNK * q + SIZE],
                forward_ref[...],
                preferred_element_type=jnp.float32,
            )
            product = scaled(product, scale)
            for k, events in enumerate(events_of(half, 0)):
                first_spec[events, q] = product[2 * k : 2 * k + 2]

    def transform_second(c, half, block):
        scale = measure(c, half, block)
        for q in range(STEPS):
            product = jnp.dot(
                held[block, c, half, :, CHUNK * q : CHUNK * q + CHUNK],
                forward_ref[:CHUNK, :],
                preferred_element_type=jnp.float32,
            )
            product = scaled(product, scale)
            for k, events in enumerate(events_of(half, block)):
                second_spec[events, q] = product[2 * k : 2 * k + 2]
        return scale

    def correlate(c):
        def one(p):
            first = slots_ref[0, 0, p]
            second = slots_ref[1, 0, p] * EVENTS + slots_ref[2, 0, p]
            real = jnp.zeros((8, SIZE // 2), jnp.float32)
            imag = jnp.zeros((8, SIZE // 2), jnp.float32)
            for q in range(STEPS):
                a = first_spec[first, q]
                b = second_spec[second, q]
                ar, ai = a[:, : SIZE // 2], a[:, SIZE // 2 :]
                br, bi = b[:, : SIZE // 2], b[:, SIZE // 2 :]
                real = real + (ar * br + ai * bi)
                imag = imag + (ai * br - ar * bi)
            rank_one[p] = nyquist[first] * nyquist[second]
            return jnp.concatenate([real, imag], axis=1)

        def some(n, carry):
            made = jnp.concatenate([one(TOGETHER * n + k) for k in range(TOGETHER)], axis=0)
            rows = pl.ds(pl.multiple_of(n * 8 * TOGETHER, 8 * TOGETHER), 8 * TOGETHER)
            cross[rows, :] = made.astype(jnp.bfloat16)
            return carry

        lax.fori_loop(0, PAIRS // TOGETHER, some, 0)
        lagged = jnp.dot(cross[...], back_ref[...], preferred_element_type=jnp.float32)
        lagged = lagged.reshape(PAIRS, 8, LAGS)
        lagged = lagged + swap_halves(lagged)
        odd = lax.rem(lax.broadcasted_iota(jnp.int32, (PAIRS, 8, 128), 2), 2)
        weight = math.sqrt(WIN) / (2 * WIN)
        term = rank_one[...] * jnp.where(odd == 0, weight, -weight)
        lagged = lagged - jnp.concatenate([term, term], axis=2)
        slot = lax.broadcasted_iota(jnp.int32, lagged.shape, 0)
        lagged = jnp.where(slot < count_ref[0], lagged, 0.0)
        out_ref[:, c] = lagged[:, :4]

    def issue(n):
        if n % 2 == 0:
            raw_copies[n // 2].wait()
            lay_out(n // 2)
        if n == 0:
            meet()
        own_copy(n).start()
        for by in ORDER:
            y_copy(n, by).start()

    def forward(n):
        for by in ORDER:
            y_copy(n, by).wait_recv()
            z_copy(n, rows_of(lax.rem(st + ST - by, ST))).start()

    def compute_own(n):
        scale = transform_second(n // 2, n % 2, 0)
        transform_first(n // 2, n % 2, scale)

    def compute_rest(n):
        z_copy(n, every).wait_recv()
        sibling_copy(n).start()
        transform_second(n // 2, n % 2, 2)
        sibling_copy(n).wait_recv()
        transform_second(n // 2, n % 2, 1)
        if n % 2:
            correlate(n // 2)

    for n in range(PIECES):
        issue(n)

    @pl.when(first)
    def _():
        pl.semaphore_wait(joined, 1)

    for n in range(PIECES):
        own_copy(n).wait()
        z_copy(n, rows_of(st)).start()
    make_tables()
    row = lax.broadcasted_iota(jnp.int32, adder.shape, 0)
    column = lax.broadcasted_iota(jnp.int32, adder.shape, 1)
    sign = 1.0 - 2.0 * lax.rem(row, 2).astype(jnp.float32)
    weight = jnp.where(row < 256, jnp.where(column < 128, 1.0, 0.0), jnp.where(column < 128, 0.0, sign))
    adder[...] = weight.astype(jnp.bfloat16)
    for n in range(PIECES):
        forward(n)
        if n:
            compute_rest(n - 1)
        compute_own(n)
    compute_rest(PIECES - 1)

    for n in range(PIECES):
        y_sent(n).wait_send()
        z_copy(n, every).wait_send()
        sibling_copy(n).wait_send()


def shards(waveforms, pair_list, pair_count):
    windows = jnp.transpose(waveforms, (0, 2, 1, 3))
    slots = jnp.transpose(pair_list, (2, 0, 1))
    whole = pl.BlockSpec(memory_space=pltpu.VMEM)
    scalar = pl.BlockSpec(memory_space=pltpu.SMEM)
    anywhere = pl.BlockSpec(memory_space=pl.ANY)
    dma = pltpu.SemaphoreType.DMA
    result = pl.pallas_call(
        kernel,
        out_shape=jax.ShapeDtypeStruct((PAIRS, COMP, STATIONS, LAGS), jnp.float32),
        in_specs=[scalar, scalar, anywhere],
        out_specs=whole,
        scratch_shapes=[
            pltpu.VMEM((SIZE, SIZE), jnp.bfloat16),
            pltpu.VMEM((SIZE, LAGS), jnp.bfloat16),
            pltpu.VMEM((OWN, COMP, ST * STATIONS, WIN), jnp.bfloat16),
            pltpu.VMEM((COMP, ST, 2, 16, HALF), jnp.bfloat16),
            pltpu.VMEM((3, COMP, 2, 16 * ST, HALF), jnp.bfloat16),
            pltpu.VMEM((ROWS // 2, HALF + 256), jnp.bfloat16),
            pltpu.VMEM((EVENTS, STEPS, 8, SIZE), jnp.float32),
            pltpu.VMEM((3 * EVENTS, STEPS, 8, SIZE), jnp.float32),
            pltpu.VMEM((3 * EVENTS, 8, 128), jnp.float32),
            pltpu.VMEM((512, 256), jnp.bfloat16),
            pltpu.VMEM((PAIRS * 8, SIZE), jnp.bfloat16),
            pltpu.VMEM((PAIRS, 8, 128), jnp.float32),
            pltpu.SemaphoreType.REGULAR,
            dma((COMP,)),
            dma((PIECES,)),
            dma((PIECES,)),
            dma((PIECES, ST)),
            dma((PIECES,)),
            dma((PIECES,)),
            dma((PIECES,)),
            dma((PIECES,)),
        ],
        compiler_params=pltpu.CompilerParams(
            collective_id=0, has_side_effects=True, vmem_limit_bytes=52 * 2**20
        ),
        name="pair_correlation",
    )(slots, pair_count, windows)
    return jnp.transpose(result, (0, 2, 1, 3))


def solution(mesh):
    in_specs = (P(("ev", "st"), None, None, None), P("ev", None, None), P("ev"))
    out_specs = P("ev", "st", None, None)
    return jax.shard_map(shards, mesh=mesh, in_specs=in_specs, out_specs=out_specs, check_vma=False)
```

```python
import math

import jax
import jax.numpy as jnp
from jax import lax
from jax.experimental import pallas as pl
from jax.experimental.pallas import tpu as pltpu
from jax.sharding import PartitionSpec as P

MESH = pl.DeviceIdType.MESH
EV, ST = 64, 8
EVENTS, OWN, STATIONS, COMP, WIN = 32, 4, 4, 3, 2048
PAIRS, LAGS = 64, 256
HALF, CHUNK, SIZE = 1024, 256, 512
STEPS = HALF // CHUNK
ROWS = EVENTS * 8
PIECES = 2 * COMP
COLUMN = 8
TOGETHER = 4
ORDER = (4, 3, 5, 2, 6, 1, 7)


def upper(shape, axis):
    return lax.broadcasted_iota(jnp.int32, shape, axis) < 4


def swap_halves(value):
    return pltpu.roll(value, 4, 1)


def kernel(
    slots_ref, count_ref, wave_ref, out_ref,
    forward_ref, back_ref, raw, parts, held, wide, first_spec, second_spec, nyquist, adder, cross, rank_one,
    joined, raw_sem, own_sem, y_send, y_recv, z_send, z_recv, s_send, s_recv,
):
    ev = lax.axis_index("ev")
    st = lax.axis_index("st")
    core = lax.rem(ev, 2)
    earlier = lax.rem(ev + EV - 2, EV)
    later = lax.rem(ev + 2, EV)
    sibling = ev + 1 - 2 * core

    raw_copies = []
    for c in range(COMP):
        copy = pltpu.make_async_copy(wave_ref.at[:, c], raw.at[:, c], raw_sem.at[c])
        copy.start()
        raw_copies.append(copy)
    barrier = pltpu.get_barrier_semaphore()
    first = lax.rem(ev // 2, COLUMN) == 0
    last = lax.rem(ev // 2, COLUMN) == COLUMN - 1
    for by in range(1, ST):
        pl.semaphore_signal(
            barrier, inc=1, device_id=(ev, lax.rem(st + by, ST)), device_id_type=MESH
        )
    pl.semaphore_signal(barrier, inc=1, device_id=(sibling, st), device_id_type=MESH)

    @pl.when(first)
    def _():
        pl.semaphore_signal(barrier, inc=1, device_id=(earlier, st), device_id_type=MESH)

    @pl.when(jnp.logical_not(last))
    def _():
        pl.semaphore_signal(barrier, inc=1, device_id=(later, st), device_id_type=MESH)

    def meet():
        before = jnp.where(first, 0, 1) + jnp.where(last, 1, 0)
        pl.semaphore_wait(barrier, ST + before)

        @pl.when(last)
        def _():
            pl.semaphore_signal(joined, inc=1, device_id=(later, st), device_id_type=MESH)

    def rows_of(source):
        return pl.ds(pl.multiple_of(source * 16, 16), 16)

    def y_copy(n, by):
        c, half = n // 2, n % 2
        target = lax.rem(st + by, ST)
        return pltpu.make_async_remote_copy(
            src_ref=parts.at[c, target, half],
            dst_ref=held.at[0, c, half, rows_of(st)],
            send_sem=y_send.at[n],
            recv_sem=y_recv.at[n, by],
            device_id=(ev, target),
            device_id_type=MESH,
        )

    def own_copy(n):
        c, half = n // 2, n % 2
        return pltpu.make_async_copy(
            parts.at[c, st, half], held.at[0, c, half, rows_of(st)], own_sem.at[n]
        )

    def z_copy(n, rows):
        c, half = n // 2, n % 2
        return pltpu.make_async_remote_copy(
            src_ref=held.at[0, c, half, rows],
            dst_ref=held.at[2, c, half, rows],
            send_sem=z_send.at[n],
            recv_sem=z_recv.at[n],
            device_id=(earlier, st),
            device_id_type=MESH,
        )

    def sibling_copy(n):
        c, half = n // 2, n % 2
        return pltpu.make_async_remote_copy(
            src_ref=held.at[2 - 2 * core, c, half],
            dst_ref=held.at[1, c, half],
            send_sem=s_send.at[n],
            recv_sem=s_recv.at[n],
            device_id=(sibling, st),
            device_id_type=MESH,
        )

    every = pl.ds(0, 16 * ST)

    def y_sent(n):
        rows = pl.ds(0, 16 * (ST - 1))
        return pltpu.make_async_remote_copy(
            src_ref=held.at[0, n // 2, n % 2, rows],
            dst_ref=held.at[0, n // 2, n % 2, rows],
            send_sem=y_send.at[n],
            recv_sem=y_recv.at[n, 0],
            device_id=(ev, lax.rem(st + 1, ST)),
            device_id_type=MESH,
        )

    def make_tables():
        def turns(rows, step):
            shape = (rows, SIZE // 2)
            odd = 2 * lax.broadcasted_iota(jnp.int32, shape, 1) + 1
            phase = lax.rem(step * lax.broadcasted_iota(jnp.int32, shape, 0) * odd, 2 * SIZE)
            angle = phase.astype(jnp.float32) * (math.pi / SIZE)
            return jnp.cos(angle), jnp.sin(angle)

        fine_cos, fine_sin = turns(16, 1)
        coarse_cos, coarse_sin = turns(SIZE // 16, 16)
        halves = [[], []]
        for n in range(SIZE // 16):
            c, s = coarse_cos[n : n + 1], coarse_sin[n : n + 1]
            cosine = c * fine_cos - s * fine_sin
            sine = -(s * fine_cos + c * fine_sin)
            rows = slice(16 * n, 16 * n + 16)
            forward_ref[rows, : SIZE // 2] = cosine.astype(jnp.bfloat16)
            forward_ref[rows, SIZE // 2 :] = sine.astype(jnp.bfloat16)
            if n < LAGS // 16:
                halves[0].append(cosine)
                halves[1].append(sine)
        weight = 2.0 / SIZE * math.sqrt(WIN)
        for k, half in enumerate(halves):
            table = weight * jnp.transpose(jnp.concatenate(half, axis=0))
            back_ref[k * (SIZE // 2) : (k + 1) * (SIZE // 2), :] = table.astype(jnp.bfloat16)

    def lay_out(c):
        def group(g, carry):
            stations = pl.ds(pl.multiple_of(g * 16, 16), 16)
            for pair in range(OWN // 2):
                for piece in range(HALF // 256):
                    low = slice(piece * 256, piece * 256 + 256)
                    high = slice(HALF + piece * 256, HALF + piece * 256 + 256)
                    made = [[], [], [], []]
                    for e in (2 * pair, 2 * pair + 1):
                        head = raw[e, c, stations, low].astype(jnp.float32)
                        tail = raw[e, c, stations, high].astype(jnp.float32)
                        for t in range(2):
                            h0 = head[8 * t : 8 * t + 8]
                            h1 = tail[8 * t : 8 * t + 8]
                            top = upper(h0.shape, 0)
                            made[2 * t].append(jnp.where(top, h0, pltpu.roll(h1, 4, 0)))
                            made[2 * t + 1].append(jnp.where(top, pltpu.roll(h0, 4, 0), h1))
                    for d in range(4):
                        both = jnp.concatenate(made[d], axis=0).astype(jnp.bfloat16)
                        parts[c, 4 * g + d, pair, :, low] = both
            return carry

        lax.fori_loop(0, 2, group, 0)

    def events_of(half, block):
        return [pl.ds(block * EVENTS + OWN * k + 2 * half, 2) for k in range(ST)]

    def measure(c, half, block):
        energy = jnp.zeros((ROWS // 2, 128), jnp.float32)
        total = jnp.zeros((ROWS // 2, 128), jnp.float32)
        for piece in range(HALF // 128):
            x = held[block, c, half, :, 128 * piece : 128 * piece + 128].astype(jnp.float32)
            energy = energy + x * x
            total = total + x
        split = []
        for value in (energy, total):
            high = value.astype(jnp.bfloat16)
            wide_high = high.astype(jnp.float32)
            rest = jnp.where(jnp.abs(wide_high) < jnp.inf, value - wide_high, 0.0)
            split += [high, rest.astype(jnp.bfloat16)]
        sums = []
        for k in range(2):
            value = jnp.dot(
                jnp.concatenate(split[2 * k : 2 * k + 2], axis=1),
                adder[256 * k : 256 * k + 256, 128 * k : 128 * k + 128],
                preferred_element_type=jnp.float32,
            ).reshape(EVENTS // 2, 8, 128)
            sums.append(value + swap_halves(value))
        scale = 1.0 / jnp.sqrt(WIN * (sums[0] * (1.0 / WIN) + 1e-6))
        alternate = sums[1] * scale
        for k, events in enumerate(events_of(half, block)):
            nyquist[events] = alternate[2 * k : 2 * k + 2]
        return scale

    def scaled(product, scale):
        product = product.reshape(scale.shape[0], 8, SIZE)
        return jnp.concatenate(
            [product[:, :, 128 * n : 128 * n + 128] * scale for n in range(SIZE // 128)], axis=2
        )

    def transform_first(c, half, scale):
        x = held[0, c, half]
        head = swap_halves(x[:, :128].astype(jnp.float32).reshape(EVENTS // 2, 8, 128))
        tail = swap_halves(x[:, HALF - 128 :].astype(jnp.float32).reshape(EVENTS // 2, 8, 128))
        top = upper(head.shape, 1)
        before = jnp.where(top, 0.0, tail).reshape(ROWS // 2, 128).astype(jnp.bfloat16)
        after = jnp.where(top, head, 0.0).reshape(ROWS // 2, 128).astype(jnp.bfloat16)
        wide[:, :128] = before
        wide[:, 128 : 128 + HALF] = x
        wide[:, 128 + HALF :] = after
        for q in range(STEPS):
            product = jnp.dot(
                wide[:, CHUNK * q : CHUNK * q + SIZE],
                forward_ref[...],
                preferred_element_type=jnp.float32,
            )
            product = scaled(product, scale)
            for k, events in enumerate(events_of(half, 0)):
                first_spec[events, q] = product[2 * k : 2 * k + 2]

    def transform_second(c, half, block):
        scale = measure(c, half, block)
        for q in range(STEPS):
            product = jnp.dot(
                held[block, c, half, :, CHUNK * q : CHUNK * q + CHUNK],
                forward_ref[:CHUNK, :],
                preferred_element_type=jnp.float32,
            )
            product = scaled(product, scale)
            for k, events in enumerate(events_of(half, block)):
                second_spec[events, q] = product[2 * k : 2 * k + 2]
        return scale

    def correlate(c):
        def one(p):
            first = slots_ref[0, 0, p]
            second = slots_ref[1, 0, p] * EVENTS + slots_ref[2, 0, p]
            real = jnp.zeros((8, SIZE // 2), jnp.float32)
            imag = jnp.zeros((8, SIZE // 2), jnp.float32)
            for q in range(STEPS):
                a = first_spec[first, q]
                b = second_spec[second, q]
                ar, ai = a[:, : SIZE // 2], a[:, SIZE // 2 :]
                br, bi = b[:, : SIZE // 2], b[:, SIZE // 2 :]
                real = real + (ar * br + ai * bi)
                imag = imag + (ai * br - ar * bi)
            rank_one[p] = nyquist[first] * nyquist[second]
            return jnp.concatenate([real, imag], axis=1)

        def some(n, carry):
            made = jnp.concatenate([one(TOGETHER * n + k) for k in range(TOGETHER)], axis=0)
            rows = pl.ds(pl.multiple_of(n * 8 * TOGETHER, 8 * TOGETHER), 8 * TOGETHER)
            cross[rows, :] = made.astype(jnp.bfloat16)
            return carry

        lax.fori_loop(0, PAIRS // TOGETHER, some, 0)
        lagged = jnp.dot(cross[...], back_ref[...], preferred_element_type=jnp.float32)
        lagged = lagged.reshape(PAIRS, 8, LAGS)
        lagged = lagged + swap_halves(lagged)
        odd = lax.rem(lax.broadcasted_iota(jnp.int32, (PAIRS, 8, 128), 2), 2)
        weight = math.sqrt(WIN) / (2 * WIN)
        term = rank_one[...] * jnp.where(odd == 0, weight, -weight)
        lagged = lagged - jnp.concatenate([term, term], axis=2)
        slot = lax.broadcasted_iota(jnp.int32, lagged.shape, 0)
        lagged = jnp.where(slot < count_ref[0], lagged, 0.0)
        out_ref[:, c] = lagged[:, :4]

    def issue(n):
        if n % 2 == 0:
            raw_copies[n // 2].wait()
            lay_out(n // 2)
        if n == 0:
            meet()
        own_copy(n).start()
        for by in ORDER:
            y_copy(n, by).start()

    def forward(n):
        for by in ORDER:
            y_copy(n, by).wait_recv()
            z_copy(n, rows_of(lax.rem(st + ST - by, ST))).start()

    def compute_own(n):
        scale = transform_second(n // 2, n % 2, 0)
        transform_first(n // 2, n % 2, scale)

    def compute_rest(n):
        z_copy(n, every).wait_recv()
        sibling_copy(n).start()
        transform_second(n // 2, n % 2, 2)
        sibling_copy(n).wait_recv()
        transform_second(n // 2, n % 2, 1)
        if n % 2:
            correlate(n // 2)

    for n in range(PIECES):
        issue(n)

    @pl.when(first)
    def _():
        pl.semaphore_wait(joined, 1)

    for n in range(PIECES):
        own_copy(n).wait()
        z_copy(n, rows_of(st)).start()
    make_tables()
    row = lax.broadcasted_iota(jnp.int32, adder.shape, 0)
    column = lax.broadcasted_iota(jnp.int32, adder.shape, 1)
    sign = 1.0 - 2.0 * lax.rem(row, 2).astype(jnp.float32)
    weight = jnp.where(row < 256, jnp.where(column < 128, 1.0, 0.0), jnp.where(column < 128, 0.0, sign))
    adder[...] = weight.astype(jnp.bfloat16)
    for n in range(PIECES):
        forward(n)
        if n:
            compute_rest(n - 1)
        compute_own(n)
    compute_rest(PIECES - 1)

    for n in range(PIECES):
        y_sent(n).wait_send()
        z_copy(n, every).wait_send()
        sibling_copy(n).wait_send()


def shards(waveforms, pair_list, pair_count):
    windows = jnp.transpose(waveforms, (0, 2, 1, 3))
    slots = jnp.transpose(pair_list, (2, 0, 1))
    whole = pl.BlockSpec(memory_space=pltpu.VMEM)
    scalar = pl.BlockSpec(memory_space=pltpu.SMEM)
    anywhere = pl.BlockSpec(memory_space=pl.ANY)
    dma = pltpu.SemaphoreType.DMA
    result = pl.pallas_call(
        kernel,
        out_shape=jax.ShapeDtypeStruct((PAIRS, COMP, STATIONS, LAGS), jnp.float32),
        in_specs=[scalar, scalar, anywhere],
        out_specs=whole,
        scratch_shapes=[
            pltpu.VMEM((SIZE, SIZE), jnp.bfloat16),
            pltpu.VMEM((SIZE, LAGS), jnp.bfloat16),
            pltpu.VMEM((OWN, COMP, ST * STATIONS, WIN), jnp.bfloat16),
            pltpu.VMEM((COMP, ST, 2, 16, HALF), jnp.bfloat16),
            pltpu.VMEM((3, COMP, 2, 16 * ST, HALF), jnp.bfloat16),
            pltpu.VMEM((ROWS // 2, HALF + 256), jnp.bfloat16),
            pltpu.VMEM((EVENTS, STEPS, 8, SIZE), jnp.float32),
            pltpu.VMEM((3 * EVENTS, STEPS, 8, SIZE), jnp.float32),
            pltpu.VMEM((3 * EVENTS, 8, 128), jnp.float32),
            pltpu.VMEM((512, 256), jnp.bfloat16),
            pltpu.VMEM((PAIRS * 8, SIZE), jnp.bfloat16),
            pltpu.VMEM((PAIRS, 8, 128), jnp.float32),
            pltpu.SemaphoreType.REGULAR,
            dma((COMP,)),
            dma((PIECES,)),
            dma((PIECES,)),
            dma((PIECES, ST)),
            dma((PIECES,)),
            dma((PIECES,)),
            dma((PIECES,)),
            dma((PIECES,)),
        ],
        compiler_params=pltpu.CompilerParams(
            collective_id=0, has_side_effects=True, vmem_limit_bytes=52 * 2**20
        ),
        name="pair_correlation",
    )(slots, pair_count, windows)
    return jnp.transpose(result, (0, 2, 1, 3))


def solution(mesh):
    in_specs = (P(("ev", "st"), None, None, None), P("ev", None, None), P("ev"))
    out_specs = P("ev", "st", None, None)
    return jax.shard_map(shards, mesh=mesh, in_specs=in_specs, out_specs=out_specs, check_vma=False)
```
